32 devices in a mesh: groups: 2 (over y), expert: 8 (over z, core), blk: 2 (over x).
Axes of the slice: x: 2, y: 2, z: 4, core: 2. Of those that a mesh axis runs over, the one named last changes fastest.
Arguments:
- tokens: bfloat16 [1536, 4096], P(('groups', 'expert'), 'blk'), parts along dimension 0, may hold values from -6 to 6
- routes: int32 [1536, 8], P(('groups', 'expert')), parts along dimension 0, may hold values from 0 to 15, all different within a row; in each aligned block of 96 rows (0 to 95, 96 to 191, ...) at most 72 rows name the same one
- route_weight: float32 [1536, 8], P(('groups', 'expert')), parts along dimension 0, may hold values from 0.05 to 0.5
- w_gate: bfloat16 [16, 4096, 1536], P(('expert', 'blk')), may hold values from -0.09375 to 0.09375
- w_up: bfloat16 [16, 4096, 1536], P(('expert', 'blk')), may hold values from -0.09375 to 0.09375
- w_down: bfloat16 [16, 1536, 4096], P(('expert', 'blk')), may hold values from -0.15625 to 0.15625
Outputs:
- moe_output: bfloat16 [1536, 4096], P(('groups', 'expert'), 'blk'), parts along dimension 0
The draws below stay inside these ranges and needn't reach their ends.
There are 2 independent parts, one for each index of `groups`. The reference program is written for one: setup_inputs(seed, part) draws one part's arguments, and reference() takes and returns one part's arrays. A program takes and returns all parts, laid end to end along the dimension named above; an argument that names none is the same for every part. Nothing has to cross between parts.
Inputs may be any that keep to these rules, and one draw needn't show every extreme that they name: `routes`: each row names 8 different experts. In the rows of one index of the expert axis (aligned blocks of 96 rows) no expert is named by more than 72 rows, a bound that some block reaches.
All inputs are finite; a program needn't handle non-finite values.
Results may differ from the reference program's by a relative error of at most 0.0057.
Values may be sent and summed in bfloat16 or wider, within the bound.
No kernel may reach another device: no remote copies, remote signals or barrier semaphores. Data moves between devices by JAX's collectives and lax.ppermute only.
A program may use at most 128 MiB of HBM per device.

```python
import math
import jax
import jax.numpy as jnp
import numpy as np
from jax import lax

D = 4096
FF = 1536
TOP = 8
TOK_E = 96
EXPERTS = 16
HSPLIT = 1
HID_DEV = 1536
TOKENS = 768
CAP = 72
N_EXPERT = 8


def block_scale(rng, dims, shards, low, largest):
    def one(axis_at, blocks):
        draws = jax.random.uniform(jax.random.fold_in(jax.random.fold_in(rng, 6), axis_at), (blocks,), jnp.float32, low / len(shards), largest / len(shards))
        return jnp.repeat(jnp.exp(draws), dims[axis_at] // blocks).reshape((-1,) + (1,) * (len(dims) - axis_at - 1))

    gain = one(*shards[0])
    for cut in shards[1:]:
        gain = gain * one(*cut)
    return gain


def deal_out(stream_key, own, number, rows, count, top, most, lean):
    sequence = jax.random.permutation(stream_key, count)
    heavy_load, ordinary = shares(count, rows * top, most, lean, True), shares(count, rows * top, most, lean, False)
    places = jnp.arange(count)

    def named(tallies, turn):
        used = int((tallies > 0).sum())
        fixed = max(1, used // 4)
        passed = fixed + (places - fixed + turn * (used - fixed)) % max(1, count - fixed)
        return jnp.zeros((count,), jnp.int32).at[sequence[jnp.where(places < fixed, places, passed)]].set(jnp.asarray(tallies, jnp.int32))

    tallies = jnp.where(number % 4 == 0, named(heavy_load, number // 4), named(ordinary, number - number // 4 - 1))
    mixed = jax.random.permutation(jax.random.fold_in(own, 3), count)
    giver, sink = mixed[0:count // 2 * 2:2], mixed[1:count // 2 * 2:2]
    room = jnp.minimum(tallies[giver] - 1, most - tallies[sink]) // 2
    room = jnp.where((giver == sequence[0]) | (sink == sequence[0]) | (tallies[sink] == 0), 0, jnp.maximum(room, 0))
    passed = jax.random.randint(jax.random.fold_in(own, 4), (count // 2,), 0, 1 << 20) % (room + 1)
    tallies = tallies.at[giver].add(-passed).at[sink].add(passed)
    items = jnp.searchsorted(jnp.cumsum(tallies), jnp.arange(rows * top), side="right").astype(jnp.int32)
    listing = items.reshape(top, rows).T
    listing = listing[jax.random.permutation(jax.random.fold_in(own, 1), rows)]
    turn = jax.random.randint(jax.random.fold_in(own, 2), (rows, 1), 0, top)
    return jnp.take_along_axis(listing, (jnp.arange(top)[None, :] + turn) % top, axis=1)


def shares(number_of, total, most, skew, full):
    portions = [(1 << 20) // math.isqrt(rank ** skew) + 1 for rank in range(1, number_of + 1)]
    largest = most if full else min(most, max(-(-total // number_of), total * portions[0] // sum(portions)))
    least = 1 if total - largest >= number_of - 1 else 0
    holding, surplus = [largest] + [least] * (number_of - 1), total - largest - least * (number_of - 1)
    while surplus > 0:
        movable = [i for i in range(1, number_of) if holding[i] < largest] or [i for i in range(1, number_of) if holding[i] < most]
        whole, remaining = sum([portions[i] for i in movable]), surplus
        for i in movable:
            more = min(most - holding[i], max(1, remaining * portions[i] // whole), surplus)
            holding[i] = holding[i] + more
            surplus = surplus - more
    return np.array(holding)


def centred(rng, dims, deviation, most, shards=(), held_as=jnp.bfloat16):
    entries = deviation * jax.random.normal(rng, dims, jnp.float32)
    if shards:
        entries = entries * block_scale(rng, dims, shards, -0.22, 0.18)
    return jnp.clip(entries, -most, most).astype(held_as)


def setup_inputs(seed: int = 0, part: int = 0) -> dict:
    key_of = jax.random.split(jax.random.key(seed), 7)
    part_splits = jax.random.split(jax.random.fold_in(key_of[6], part), 7)
    tokens = centred(part_splits[0], (TOKENS, D), 1.0, 6.0, ((0, 8), (1, 2)))
    routes_keys = jax.random.split(jax.random.fold_in(part_splits[1], 1), TOKENS // TOK_E)
    routes_turns = jax.random.permutation(jax.random.fold_in(part_splits[1], 3), TOKENS // TOK_E)
    routes = jax.vmap(lambda own, number: deal_out(jax.random.fold_in(part_splits[1], 2), own, number, TOK_E, EXPERTS, TOP, CAP, 1))(routes_keys, routes_turns).reshape((TOKENS, TOP))
    route_weight = jnp.clip(jnp.exp(math.log(0.5) - 2.3025851 * jax.random.uniform(part_splits[2], (TOKENS, TOP), jnp.float32) ** block_scale(part_splits[2], (TOKENS, TOP), ((0, 8),), -0.2, 0.2)), 0.05, 0.5)
    w_gate = centred(key_of[3], (EXPERTS * HSPLIT, D, HID_DEV), D ** -0.5, 0.09375, ((0, 16),))
    w_up = centred(key_of[4], (EXPERTS * HSPLIT, D, HID_DEV), D ** -0.5, 0.09375, ((0, 16),))
    w_down = centred(key_of[5], (EXPERTS * HSPLIT, HID_DEV, D), FF ** -0.5, 0.15625, ((0, 16),))
    return dict(tokens=tokens, routes=routes, route_weight=route_weight, w_gate=w_gate, w_up=w_up, w_down=w_down)


def reference(tokens, routes, route_weight, w_gate, w_up, w_down):
    tokens_all, top = routes.shape
    width = tokens.shape[1]
    hid_block = w_gate.shape[2]
    limit = N_EXPERT * CAP
    flat = routes.reshape(-1)
    weights_flat = route_weight.reshape(-1)

    def one_expert(total, expert_id):
        keys = (flat != expert_id).astype(jnp.int32)
        order = jnp.argsort(keys, stable=True)[:limit].astype(jnp.int32)
        valid = flat[order] == expert_id
        owners = (order // top).astype(jnp.int32)
        rows = tokens[owners]
        first = (expert_id * HSPLIT).astype(jnp.int32)
        gate_w = lax.dynamic_slice_in_dim(w_gate, first, HSPLIT, 0)
        up_w = lax.dynamic_slice_in_dim(w_up, first, HSPLIT, 0)
        down_w = lax.dynamic_slice_in_dim(w_down, first, HSPLIT, 0)
        gate_full = jnp.transpose(gate_w, (1, 0, 2)).reshape(width, HSPLIT * hid_block)
        up_full = jnp.transpose(up_w, (1, 0, 2)).reshape(width, HSPLIT * hid_block)
        gate = jnp.dot(rows, gate_full, preferred_element_type=jnp.float32)
        upward = jnp.dot(rows, up_full, preferred_element_type=jnp.float32)
        hidden = (jax.nn.silu(gate) * upward).astype(jnp.bfloat16)
        blocks = hidden.astype(jnp.float32).reshape(limit, HSPLIT, hid_block)
        parts = jnp.einsum("rbh,bhd->rbd", blocks, down_w.astype(jnp.float32)).astype(jnp.bfloat16)
        scale = jnp.where(valid, weights_flat[order], jnp.zeros_like(weights_flat[order]))
        contrib = jnp.sum(parts.astype(jnp.float32), axis=1) * scale[:, None]
        return total.at[owners].add(contrib), None

    start = jnp.zeros((tokens_all, width), jnp.float32)
    total, _ = lax.scan(one_expert, start, jnp.arange(EXPERTS, dtype=jnp.int32))
    return total.astype(jnp.bfloat16)
```

```python
import functools

import jax
import jax.numpy as jnp
from jax import lax
from jax.experimental import pallas as pl
from jax.experimental.pallas import tpu as pltpu
from jax.sharding import PartitionSpec as P

EXP_DEV = 2
CORES = 2


def ffn_kernel(n_parts, n_up, pos_ref, *refs):
    pieces = refs[: CORES * n_parts]
    scale_ref, gate_ref, up_ref, down_ref, own_ref, other_ref, rows_ref, hidden_ref = refs[CORES * n_parts :]
    step = pl.program_id(0)
    tok, width = pieces[0].shape
    block = gate_ref.shape[2]

    @pl.when(step == 0)
    def _():
        for core in range(CORES):
            for part in range(n_parts):
                rows_ref[part, core * tok : (core + 1) * tok, :] = pieces[core * n_parts + part][...]

    @pl.when(step < n_up)
    def _():
        gate = upward = None
        for part in range(n_parts):
            first = pl.ds(pl.multiple_of(pos_ref[CORES + part], width), width)
            g = jnp.dot(rows_ref[part], gate_ref[0, first, :], preferred_element_type=jnp.float32)
            u = jnp.dot(rows_ref[part], up_ref[0, first, :], preferred_element_type=jnp.float32)
            gate = g if gate is None else gate + g
            upward = u if upward is None else upward + u
        hidden = (gate / (1.0 + jnp.exp(-gate)) * upward).astype(jnp.bfloat16)
        hidden_ref[step] = hidden

    @pl.when(step >= n_up)
    def _():
        out = None
        for part in range(n_up):
            o = jnp.dot(hidden_ref[part], down_ref[0, part * block : (part + 1) * block, :], preferred_element_type=jnp.float32)
            out = o if out is None else out + o
        here = lax.broadcasted_iota(jnp.int32, (tok, tok), 0) == lax.broadcasted_iota(jnp.int32, (tok, tok), 1)
        for core, out_ref in enumerate((own_ref, other_ref)):
            row = scale_ref[pl.ds(pos_ref[core], 1), :]
            column = jnp.sum(jnp.where(here, row, 0.0), axis=1, keepdims=True)
            out_ref[0] = (out[core * tok : (core + 1) * tok] * column).astype(jnp.bfloat16)


def ffn(pos, pieces, scale, w_gate, w_up, w_down):
    n_parts = len(pieces[0])
    tok, width = pieces[0][0].shape
    feats, hid = w_gate.shape[1:]
    block = 256 if hid % 256 == 0 else hid
    wide = min(512, width)
    n_up, n_down, per = hid // block, feats // wide, width // wide
    rows = CORES * tok

    def down_map(step, pos_ref):
        at = jnp.maximum(step - n_up, 0)
        return (0, 0, pos_ref[CORES + at // per] // wide + at % per)

    def out_map(step, pos_ref):
        at = jnp.maximum(step - n_up, 0)
        return (at // per, 0, at % per)

    up_spec = pl.BlockSpec((1, feats, block), lambda step, pos_ref: (0, 0, jnp.minimum(step, n_up - 1)))
    whole = lambda array: pl.BlockSpec(array.shape, lambda step, pos_ref: (0,) * array.ndim)
    flat = [piece for row in pieces for piece in row]
    out_spec = pl.BlockSpec((1, tok, wide), out_map)
    out_shape = jax.ShapeDtypeStruct((n_parts, tok, width), jnp.bfloat16)
    return pl.pallas_call(
        functools.partial(ffn_kernel, n_parts, n_up),
        grid_spec=pltpu.PrefetchScalarGridSpec(
            num_scalar_prefetch=1,
            grid=(n_up + n_down,),
            in_specs=[whole(piece) for piece in flat]
            + [whole(scale), up_spec, up_spec, pl.BlockSpec((1, hid, wide), down_map)],
            out_specs=[out_spec, out_spec],
            scratch_shapes=[
                pltpu.VMEM((n_parts, rows, width), jnp.bfloat16),
                pltpu.VMEM((n_up, rows, block), jnp.bfloat16),
            ],
        ),
        out_shape=[out_shape, out_shape],
        compiler_params=pltpu.CompilerParams(vmem_limit_bytes=40 * 1024 * 1024),
        cost_estimate=pl.CostEstimate(
            flops=6 * rows * feats * hid, bytes_accessed=6 * feats * hid + 4 * rows * feats, transcendentals=rows * hid
        ),
    )(pos, *flat, scale, w_gate, w_up, w_down)


def on_device(tokens, routes, route_weight, w_gate, w_up, w_down):
    tok = routes.shape[0]
    members, blks = lax.axis_size("expert"), lax.axis_size("blk")
    chips = members // CORES
    split = blks // EXP_DEV
    me, blk = lax.axis_index("expert"), lax.axis_index("blk")
    width = tokens.shape[1]
    pair = blks == 2

    def partner(index, chip):
        return (index // CORES ^ chip) * CORES + index % CORES

    def to_chip(value, chip):
        return lax.ppermute(value, "expert", [(i, partner(i, chip)) for i in range(members)])

    def to_core(value):
        return lax.ppermute(value, "expert", [(i, i ^ 1) for i in range(members)])

    def to_blk(value):
        return lax.ppermute(value, "blk", [(0, 1), (1, 0)])

    f32, bf16 = jnp.float32, jnp.bfloat16
    arrived = [tokens] + [to_chip(tokens, k) for k in range(1, chips)]
    mine = jnp.arange(members, dtype=jnp.int32) * EXP_DEV + blk // split
    shares = jnp.sum(jnp.where(routes[None] == mine[:, None, None], route_weight[None], 0.0), axis=2)
    scale = lax.all_to_all(shares, "expert", split_axis=0, concat_axis=0, tiled=True)

    firsts = [blk * width, (1 - blk) * width] if pair else [jnp.zeros_like(blk)]
    total = None
    outs = []
    for k in range(chips):
        piece = arrived[k]
        own = [piece, to_blk(piece)] if pair else [lax.all_gather(piece, "blk", axis=1, tiled=True)]
        pos = jnp.stack([me ^ (CORES * k), me ^ (CORES * k + 1)] + firsts).astype(jnp.int32)
        outs.append(ffn(pos, [own, [to_core(v) for v in own]], scale, w_gate, w_up, w_down))
    for k in range(chips):
        kept, sent = outs[k]
        part = kept.astype(f32) + to_core(sent).astype(f32)
        if pair:
            part = part[0] + to_blk(part[1].astype(bf16)).astype(f32)
        else:
            part = lax.psum_scatter(part[0], "blk", scatter_dimension=1, tiled=True)
        if k:
            part = to_chip(part.astype(bf16), k).astype(f32)
        total = part if total is None else total + part
    return total.astype(bf16)


def solution(mesh):
    in_specs = (
        P(("groups", "expert"), "blk"),
        P(("groups", "expert"), None),
        P(("groups", "expert"), None),
        P(("expert", "blk"), None, None),
        P(("expert", "blk"), None, None),
        P(("expert", "blk"), None, None),
    )
    out_specs = P(("groups", "expert"), "blk")
    return jax.shard_map(
        on_device, mesh=mesh, in_specs=in_specs, out_specs=out_specs, check_vma=False
    )
```

```python
import functools

import jax
import jax.numpy as jnp
from jax import lax
from jax.experimental import pallas as pl
from jax.experimental.pallas import tpu as pltpu
from jax.sharding import PartitionSpec as P

EXP_DEV = 2
CORES = 2
f32, bf16 = jnp.float32, jnp.bfloat16
VMEM_LIMIT = 48 * 1024 * 1024


def after(value, *earlier):
    return lax.optimization_barrier((value, *earlier))[0]


def hidden_kernel(n_blocks, n_parts, pos_ref, *refs):
    pieces = refs[: n_blocks * n_parts]
    gate_ref, up_ref, out_ref, rows_ref = refs[n_blocks * n_parts :]
    tok, width = pieces[0].shape

    @pl.when(pl.program_id(0) == 0)
    def _():
        for at in range(n_blocks):
            for part in range(n_parts):
                rows_ref[part, at * tok : (at + 1) * tok, :] = pieces[at * n_parts + part][...]

    gate = upward = None
    for part in range(n_parts):
        first = pl.ds(pl.multiple_of(pos_ref[part], width), width)
        g = jnp.dot(rows_ref[part], gate_ref[0, first, :], preferred_element_type=f32)
        u = jnp.dot(rows_ref[part], up_ref[0, first, :], preferred_element_type=f32)
        gate = g if gate is None else gate + g
        upward = u if upward is None else upward + u
    out_ref[...] = (gate / (1.0 + jnp.exp(-gate)) * upward).astype(bf16)


def hidden_units(pos, blocks, w_gate, w_up, start, stop, unit):
    n_parts = len(blocks[0])
    tok, width = blocks[0][0].shape
    feats = w_gate.shape[1]
    rows = len(blocks) * tok
    flat = [piece for block in blocks for piece in block]
    up_spec = pl.BlockSpec((1, feats, unit), lambda step, pos_ref: (0, 0, start // unit + step))
    whole = lambda array: pl.BlockSpec(array.shape, lambda step, pos_ref: (0,) * array.ndim)
    return pl.pallas_call(
        functools.partial(hidden_kernel, len(blocks), n_parts),
        grid_spec=pltpu.PrefetchScalarGridSpec(
            num_scalar_prefetch=1,
            grid=((stop - start) // unit,),
            in_specs=[whole(piece) for piece in flat] + [up_spec, up_spec],
            out_specs=pl.BlockSpec((rows, unit), lambda step, pos_ref: (0, step)),
            scratch_shapes=[pltpu.VMEM((n_parts, rows, width), bf16)],
        ),
        out_shape=jax.ShapeDtypeStruct((rows, stop - start), bf16),
        compiler_params=pltpu.CompilerParams(vmem_limit_bytes=VMEM_LIMIT),
        cost_estimate=pl.CostEstimate(
            flops=4 * rows * feats * (stop - start),
            bytes_accessed=4 * feats * (stop - start) + 2 * rows * feats,
            transcendentals=rows * (stop - start),
        ),
    )(pos, *flat, w_gate, w_up)


def down_kernel(n_hidden, pos_ref, *refs):
    hidden = refs[:n_hidden]
    scale_ref, down_ref = refs[n_hidden : n_hidden + 2]
    outs = refs[n_hidden + 2 :]
    tok = outs[0].shape[0]
    out, first = None, 0
    for h_ref in hidden:
        o = jnp.dot(h_ref[...], down_ref[0, first : first + h_ref.shape[1], :], preferred_element_type=f32)
        out = o if out is None else out + o
        first += h_ref.shape[1]
    here = lax.broadcasted_iota(jnp.int32, (tok, tok), 0) == lax.broadcasted_iota(jnp.int32, (tok, tok), 1)
    for at, out_ref in enumerate(outs):
        row = scale_ref[pl.ds(pos_ref[1 + at], 1), :]
        column = jnp.sum(jnp.where(here, row, 0.0), axis=1, keepdims=True)
        out_ref[...] = (out[at * tok : (at + 1) * tok] * column).astype(bf16)


def down_units(pos, hidden, scale, w_down, tok, width):
    hid = w_down.shape[1]
    rows = hidden[0].shape[0]
    wide = min(1024, width)
    whole = lambda array: pl.BlockSpec(array.shape, lambda step, pos_ref: (0,) * array.ndim)
    out_spec = pl.BlockSpec((tok, wide), lambda step, pos_ref: (0, step))
    n_out = rows // tok
    return pl.pallas_call(
        functools.partial(down_kernel, len(hidden)),
        grid_spec=pltpu.PrefetchScalarGridSpec(
            num_scalar_prefetch=1,
            grid=(width // wide,),
            in_specs=[whole(h) for h in hidden]
            + [whole(scale), pl.BlockSpec((1, hid, wide), lambda step, pos_ref: (0, 0, pos_ref[0] // wide + step))],
            out_specs=[out_spec] * n_out,
        ),
        out_shape=[jax.ShapeDtypeStruct((tok, width), bf16)] * n_out,
        compiler_params=pltpu.CompilerParams(vmem_limit_bytes=VMEM_LIMIT),
        cost_estimate=pl.CostEstimate(
            flops=2 * rows * width * hid, bytes_accessed=2 * width * hid + 2 * rows * (width + hid), transcendentals=0
        ),
    )(pos, *hidden, scale, w_down)


def on_device(tokens, routes, route_weight, w_gate, w_up, w_down):
    tok = routes.shape[0]
    members, blks = lax.axis_size("expert"), lax.axis_size("blk")
    chips = members // CORES
    split = blks // EXP_DEV
    me, blk = lax.axis_index("expert"), lax.axis_index("blk")
    hid, feats = w_down.shape[1:]
    pair = blks == 2
    width = tokens.shape[1] if pair else feats
    bits = [1 << i for i in range((chips - 1).bit_length())]

    def to_chip(value, chip):
        return lax.ppermute(value, "expert", [(i, i ^ (CORES * chip)) for i in range(members)])

    def to_core(value):
        return lax.ppermute(value, "expert", [(i, i ^ 1) for i in range(members)])

    def to_blk(value):
        return lax.ppermute(value, "blk", [(0, 1), (1, 0)])

    arrived = {0: tokens}
    for bit in bits[::-1]:
        for k in list(arrived):
            arrived[k ^ bit] = to_chip(arrived[k], bit)
    mine = jnp.arange(members, dtype=jnp.int32) * EXP_DEV + blk // split
    shares = jnp.sum(jnp.where(routes[None] == mine[:, None, None], route_weight[None], 0.0), axis=2)
    scale = lax.all_to_all(shares, "expert", split_axis=0, concat_axis=0, tiled=True)

    firsts = [blk * width, (1 - blk) * width] if pair else [jnp.zeros_like(blk)]
    groups = [(k, k + 1) for k in range(0, chips, 2)] if chips % 2 == 0 else [(k,) for k in range(chips)]
    unit = 512 if hid % 512 == 0 else hid
    pos = after(jnp.stack(firsts).astype(jnp.int32), scale)
    hidden, done = [], None
    for at, group in enumerate(groups):
        blocks = []
        for k in group:
            piece = arrived[k]
            if done is not None and k == group[-1]:
                piece = after(piece, done)
            own = [piece, to_blk(piece)] if pair else [lax.all_gather(piece, "blk", axis=1, tiled=True)]
            blocks += [own, [to_core(v) for v in own]]
        cuts = [0, unit, hid] if at == 0 and unit < hid else [0, hid]
        hidden.append([])
        for a, b in zip(cuts[:-1], cuts[1:]):
            hidden[-1].append(hidden_units(pos, blocks, w_gate, w_up, a, b, unit))
            pos = after(pos, hidden[-1][-1])
        done = hidden[-1][0]

    sums, done = {}, None
    for at in range(len(groups))[::-1]:
        group = groups[at]
        rows_of = [me ^ (CORES * k + core) for k in group for core in range(CORES)]
        outs = {}
        for part in range(len(firsts))[::-1]:
            where = jnp.stack([firsts[part]] + rows_of).astype(jnp.int32)
            if done is not None:
                where = after(where, *done)
            outs[part] = down_units(where, hidden[at], scale, w_down, tok, width)
            done = list(outs[part])
        over = {}
        for part in outs:
            for i in range(len(group))[::-1]:
                kept, sent = outs[part][CORES * i], outs[part][CORES * i + 1]
                over[part, i] = kept.astype(f32) + to_core(sent).astype(f32)
                if part:
                    over[part, i] = over[part, i].astype(bf16)
                    done = done + [over[part, i]]
        for i in range(len(group))[::-1]:
            if pair:
                sums[group[i]] = over[0, i] + to_blk(over[1, i]).astype(f32)
            else:
                sums[group[i]] = lax.psum_scatter(over[0, i], "blk", scatter_dimension=1, tiled=True)
    for bit in bits:
        for k in sorted(sums, reverse=True):
            if k & bit:
                sums[k ^ bit] = sums[k ^ bit] + to_chip(sums.pop(k).astype(bf16), bit).astype(f32)
    return sums[0].astype(bf16)


def solution(mesh):
    in_specs = (
        P(("groups", "expert"), "blk"),
        P(("groups", "expert"), None),
        P(("groups", "expert"), None),
        P(("expert", "blk"), None, None),
        P(("expert", "blk"), None, None),
        P(("expert", "blk"), None, None),
    )
    out_specs = P(("groups", "expert"), "blk")
    return jax.shard_map(
        on_device, mesh=mesh, in_specs=in_specs, out_specs=out_specs, check_vma=False
    )
```

```python
import functools

import jax
import jax.numpy as jnp
from jax import lax
from jax.experimental import pallas as pl
from jax.experimental.pallas import tpu as pltpu
from jax.sharding import PartitionSpec as P

EXP_DEV = 2
CORES = 2
f32, bf16 = jnp.float32, jnp.bfloat16
VMEM_LIMIT = 52 * 1024 * 1024


def after(value, *earlier):
    return lax.optimization_barrier((value, *earlier))[0]


def hidden_kernel(n_blocks, n_parts, pos_ref, *refs):
    pieces = refs[: n_blocks * n_parts]
    gate_ref, up_ref, out_ref, rows_ref = refs[n_blocks * n_parts :]
    tok, width = pieces[0].shape

    @pl.when(pl.program_id(0) == 0)
    def _():
        for at in range(n_blocks):
            for part in range(n_parts):
                rows_ref[part, at * tok : (at + 1) * tok, :] = pieces[at * n_parts + part][...]

    gate = upward = None
    for part in range(n_parts):
        first = pl.ds(pl.multiple_of(pos_ref[part], width), width)
        g = jnp.dot(rows_ref[part], gate_ref[0, first, :], preferred_element_type=f32)
        u = jnp.dot(rows_ref[part], up_ref[0, first, :], preferred_element_type=f32)
        gate = g if gate is None else gate + g
        upward = u if upward is None else upward + u
    out_ref[...] = (gate / (1.0 + jnp.exp(-gate)) * upward).astype(bf16)


def hidden_units(pos, blocks, w_gate, w_up, start, stop, unit):
    n_parts = len(blocks[0])
    tok, width = blocks[0][0].shape
    feats = w_gate.shape[1]
    rows = len(blocks) * tok
    flat = [piece for block in blocks for piece in block]
    up_spec = pl.BlockSpec((1, feats, unit), lambda step, pos_ref: (0, 0, start // unit + step))
    whole = lambda array: pl.BlockSpec(array.shape, lambda step, pos_ref: (0,) * array.ndim)
    return pl.pallas_call(
        functools.partial(hidden_kernel, len(blocks), n_parts),
        grid_spec=pltpu.PrefetchScalarGridSpec(
            num_scalar_prefetch=1,
            grid=((stop - start) // unit,),
            in_specs=[whole(piece) for piece in flat] + [up_spec, up_spec],
            out_specs=pl.BlockSpec((rows, unit), lambda step, pos_ref: (0, step)),
            scratch_shapes=[pltpu.VMEM((n_parts, rows, width), bf16)],
        ),
        out_shape=jax.ShapeDtypeStruct((rows, stop - start), bf16),
        compiler_params=pltpu.CompilerParams(vmem_limit_bytes=VMEM_LIMIT),
        cost_estimate=pl.CostEstimate(
            flops=4 * rows * feats * (stop - start),
            bytes_accessed=4 * feats * (stop - start) + 2 * rows * feats,
            transcendentals=rows * (stop - start),
        ),
    )(pos, *flat, w_gate, w_up)


def down_kernel(n_hidden, pos_ref, *refs):
    hidden = refs[:n_hidden]
    scale_ref, down_ref = refs[n_hidden : n_hidden + 2]
    outs = refs[n_hidden + 2 :]
    tok = outs[0].shape[0]
    out, first = None, 0
    for h_ref in hidden:
        o = jnp.dot(h_ref[...], down_ref[0, first : first + h_ref.shape[1], :], preferred_element_type=f32)
        out = o if out is None else out + o
        first += h_ref.shape[1]
    here = lax.broadcasted_iota(jnp.int32, (tok, tok), 0) == lax.broadcasted_iota(jnp.int32, (tok, tok), 1)
    for at, out_ref in enumerate(outs):
        row = scale_ref[pl.ds(pos_ref[1 + at], 1), :]
        column = jnp.sum(jnp.where(here, row, 0.0), axis=1, keepdims=True)
        out_ref[...] = (out[at * tok : (at + 1) * tok] * column).astype(bf16)


def down_units(pos, hidden, scale, w_down, tok, width):
    hid = w_down.shape[1]
    rows = hidden[0].shape[0]
    wide = min(1024, width)
    whole = lambda array: pl.BlockSpec(array.shape, lambda step, pos_ref: (0,) * array.ndim)
    out_spec = pl.BlockSpec((tok, wide), lambda step, pos_ref: (0, step))
    n_out = rows // tok
    return pl.pallas_call(
        functools.partial(down_kernel, len(hidden)),
        grid_spec=pltpu.PrefetchScalarGridSpec(
            num_scalar_prefetch=1,
            grid=(width // wide,),
            in_specs=[whole(h) for h in hidden]
            + [whole(scale), pl.BlockSpec((1, hid, wide), lambda step, pos_ref: (0, 0, pos_ref[0] // wide + step))],
            out_specs=[out_spec] * n_out,
        ),
        out_shape=[jax.ShapeDtypeStruct((tok, width), bf16)] * n_out,
        compiler_params=pltpu.CompilerParams(vmem_limit_bytes=VMEM_LIMIT),
        cost_estimate=pl.CostEstimate(
            flops=2 * rows * width * hid, bytes_accessed=2 * width * hid + 2 * rows * (width + hid), transcendentals=0
        ),
    )(pos, *hidden, scale, w_down)


def on_device(tokens, routes, route_weight, w_gate, w_up, w_down):
    tok = routes.shape[0]
    members, blks = lax.axis_size("expert"), lax.axis_size("blk")
    chips = members // CORES
    split = blks // EXP_DEV
    me, blk = lax.axis_index("expert"), lax.axis_index("blk")
    hid, feats = w_down.shape[1:]
    pair = blks == 2
    width = tokens.shape[1] if pair else feats
    bits = [1 << i for i in range((chips - 1).bit_length())]

    def to_chip(value, chip):
        return lax.ppermute(value, "expert", [(i, i ^ (CORES * chip)) for i in range(members)])

    def to_core(value):
        return lax.ppermute(value, "expert", [(i, i ^ 1) for i in range(members)])

    def to_blk(value):
        return lax.ppermute(value, "blk", [(0, 1), (1, 0)])

    arrived = {0: tokens}
    for bit in bits[::-1]:
        for k in list(arrived):
            arrived[k ^ bit] = to_chip(arrived[k], bit)
    mine = jnp.arange(members, dtype=jnp.int32) * EXP_DEV + blk // split
    shares = jnp.sum(jnp.where(routes[None] == mine[:, None, None], route_weight[None], 0.0), axis=2)
    scale = lax.all_to_all(shares, "expert", split_axis=0, concat_axis=0, tiled=True)

    firsts = [blk * width, (1 - blk) * width] if pair else [jnp.zeros_like(blk)]
    groups = [(k, k + 1) for k in range(0, chips, 2)] if chips % 2 == 0 else [(k,) for k in range(chips)]
    unit = 512 if hid % 512 == 0 else hid
    pos = jnp.stack(firsts).astype(jnp.int32)
    hidden, held = [], None
    for at, group in enumerate(groups):
        blocks = []
        for k in group:
            piece = arrived[k]
            own = [piece, to_blk(piece)] if pair else [lax.all_gather(piece, "blk", axis=1, tiled=True)]
            if at:
                own[-1] = after(own[-1], held)
            elif k == group[-1]:
                own[-1] = after(own[-1], scale, arrived[groups[-1][-1]])
            blocks += [own, [to_core(v) for v in own]]
        cuts = [0, hid]
        hidden.append([])
        for a, b in zip(cuts[:-1], cuts[1:]):
            hidden[-1].append(hidden_units(pos, blocks, w_gate, w_up, a, b, unit))
            pos = after(pos, hidden[-1][-1])
        held = hidden[-1][0]

    sums, done, last = {}, [pos], None
    for at in range(len(groups))[::-1]:
        group = groups[at]
        rows_of = [me ^ (CORES * k + core) for k in group for core in range(CORES)]
        over = {}
        for part in range(len(firsts))[::-1]:
            where = jnp.stack([firsts[part]] + rows_of).astype(jnp.int32)
            if not part and last is not None:
                done.append(first_sum)
            elif last is not None:
                done += handed
            outs = down_units(after(where, *done), hidden[at], scale, w_down, tok, width)
            done = list(outs)
            for i in range(len(group))[::-1]:
                total = outs[CORES * i].astype(f32) + to_core(outs[CORES * i + 1]).astype(f32)
                over[part, i] = total.astype(bf16) if part else total
            if part and last is None:
                handed = [over[part, i] for i in range(len(group))]
        for i in range(len(group))[::-1]:
            if pair:
                came = to_blk(over[1, i] if last is None else after(over[1, i], last))
                last = over[0, i] + came.astype(f32)
                if not sums:
                    first_sum = last = last.astype(bf16)
                sums[group[i]] = last
            else:
                sums[group[i]] = lax.psum_scatter(over[0, i], "blk", scatter_dimension=1, tiled=True)
    for bit in bits:
        for k in sorted(sums, reverse=True):
            if k & bit:
                sums[k ^ bit] = sums[k ^ bit] + to_chip(sums.pop(k).astype(bf16), bit).astype(f32)
    return sums[0].astype(bf16)


def solution(mesh):
    in_specs = (
        P(("groups", "expert"), "blk"),
        P(("groups", "expert"), None),
        P(("groups", "expert"), None),
        P(("expert", "blk"), None, None),
        P(("expert", "blk"), None, None),
        P(("expert", "blk"), None, None),
    )
    out_specs = P(("groups", "expert"), "blk")
    return jax.shard_map(
        on_device, mesh=mesh, in_specs=in_specs, out_specs=out_specs, check_vma=False
    )
```

```python
import functools

import jax
import jax.numpy as jnp
from jax import lax
from jax.experimental import pallas as pl
from jax.experimental.pallas import tpu as pltpu
from jax.sharding import PartitionSpec as P

EXP_DEV = 2
CORES = 2
f32, bf16 = jnp.float32, jnp.bfloat16
VMEM_LIMIT = 52 * 1024 * 1024


def after(value, *earlier):
    return lax.optimization_barrier((value, *earlier))[0]


def hidden_kernel(n_blocks, n_parts, pos_ref, *refs):
    pieces = refs[: n_blocks * n_parts]
    gate_ref, up_ref, out_ref, rows_ref = refs[n_blocks * n_parts :]
    tok, width = pieces[0].shape

    @pl.when(pl.program_id(0) == 0)
    def _():
        for at in range(n_blocks):
            for part in range(n_parts):
                rows_ref[part, at * tok : (at + 1) * tok, :] = pieces[at * n_parts + part][...]

    gate = upward = None
    for part in range(n_parts):
        first = pl.ds(pl.multiple_of(pos_ref[part], width), width)
        g = jnp.dot(rows_ref[part], gate_ref[0, first, :], preferred_element_type=f32)
        u = jnp.dot(rows_ref[part], up_ref[0, first, :], preferred_element_type=f32)
        gate = g if gate is None else gate + g
        upward = u if upward is None else upward + u
    out_ref[...] = (gate / (1.0 + jnp.exp(-gate)) * upward).astype(bf16)


def hidden_units(pos, blocks, w_gate, w_up, start, stop, unit):
    n_parts = len(blocks[0])
    tok, width = blocks[0][0].shape
    feats = w_gate.shape[1]
    rows = len(blocks) * tok
    flat = [piece for block in blocks for piece in block]
    up_spec = pl.BlockSpec((1, feats, unit), lambda step, pos_ref: (0, 0, start // unit + step))
    whole = lambda array: pl.BlockSpec(array.shape, lambda step, pos_ref: (0,) * array.ndim)
    return pl.pallas_call(
        functools.partial(hidden_kernel, len(blocks), n_parts),
        grid_spec=pltpu.PrefetchScalarGridSpec(
            num_scalar_prefetch=1,
            grid=((stop - start) // unit,),
            in_specs=[whole(piece) for piece in flat] + [up_spec, up_spec],
            out_specs=pl.BlockSpec((rows, unit), lambda step, pos_ref: (0, step)),
            scratch_shapes=[pltpu.VMEM((n_parts, rows, width), bf16)],
        ),
        out_shape=jax.ShapeDtypeStruct((rows, stop - start), bf16),
        compiler_params=pltpu.CompilerParams(vmem_limit_bytes=VMEM_LIMIT),
        cost_estimate=pl.CostEstimate(
            flops=4 * rows * feats * (stop - start),
            bytes_accessed=4 * feats * (stop - start) + 2 * rows * feats,
            transcendentals=rows * (stop - start),
        ),
    )(pos, *flat, w_gate, w_up)


def down_kernel(n_hidden, pos_ref, *refs):
    hidden = refs[:n_hidden]
    scale_ref, down_ref = refs[n_hidden : n_hidden + 2]
    outs = refs[n_hidden + 2 :]
    tok = outs[0].shape[0]
    out, first = None, 0
    for h_ref in hidden:
        o = jnp.dot(h_ref[...], down_ref[0, first : first + h_ref.shape[1], :], preferred_element_type=f32)
        out = o if out is None else out + o
        first += h_ref.shape[1]
    here = lax.broadcasted_iota(jnp.int32, (tok, tok), 0) == lax.broadcasted_iota(jnp.int32, (tok, tok), 1)
    for at, out_ref in enumerate(outs):
        row = scale_ref[pl.ds(pos_ref[1 + at], 1), :]
        column = jnp.sum(jnp.where(here, row, 0.0), axis=1, keepdims=True)
        out_ref[...] = (out[at * tok : (at + 1) * tok] * column).astype(bf16)


def down_units(pos, hidden, scale, w_down, tok, width):
    hid = w_down.shape[1]
    rows = hidden[0].shape[0]
    wide = min(1024, width)
    whole = lambda array: pl.BlockSpec(array.shape, lambda step, pos_ref: (0,) * array.ndim)
    out_spec = pl.BlockSpec((tok, wide), lambda step, pos_ref: (0, step))
    n_out = rows // tok
    return pl.pallas_call(
        functools.partial(down_kernel, len(hidden)),
        grid_spec=pltpu.PrefetchScalarGridSpec(
            num_scalar_prefetch=1,
            grid=(width // wide,),
            in_specs=[whole(h) for h in hidden]
            + [whole(scale), pl.BlockSpec((1, hid, wide), lambda step, pos_ref: (0, 0, pos_ref[0] // wide + step))],
            out_specs=[out_spec] * n_out,
        ),
        out_shape=[jax.ShapeDtypeStruct((tok, width), bf16)] * n_out,
        compiler_params=pltpu.CompilerParams(vmem_limit_bytes=VMEM_LIMIT),
        cost_estimate=pl.CostEstimate(
            flops=2 * rows * width * hid, bytes_accessed=2 * width * hid + 2 * rows * (width + hid), transcendentals=0
        ),
    )(pos, *hidden, scale, w_down)


def on_device(tokens, routes, route_weight, w_gate, w_up, w_down):
    tok = routes.shape[0]
    members, blks = lax.axis_size("expert"), lax.axis_size("blk")
    chips = members // CORES
    split = blks // EXP_DEV
    me, blk = lax.axis_index("expert"), lax.axis_index("blk")
    hid, feats = w_down.shape[1:]
    pair = blks == 2
    width = tokens.shape[1] if pair else feats
    bits = [1 << i for i in range((chips - 1).bit_length())]

    def to_chip(value, chip):
        return lax.ppermute(value, "expert", [(i, i ^ (CORES * chip)) for i in range(members)])

    def to_core(value):
        return lax.ppermute(value, "expert", [(i, i ^ 1) for i in range(members)])

    def to_blk(value):
        return lax.ppermute(value, "blk", [(0, 1), (1, 0)])

    mine = jnp.arange(members, dtype=jnp.int32) * EXP_DEV + blk // split
    shares = jnp.sum(jnp.where(routes[None] == mine[:, None, None], route_weight[None], 0.0), axis=2)
    scale = lax.all_to_all(shares, "expert", split_axis=0, concat_axis=0, tiled=True)
    arrived = {0: tokens}
    for bit in bits[::-1]:
        for k in list(arrived):
            arrived[k ^ bit] = to_chip(arrived[k], bit)
    arrived[1] = after(arrived[1], shares)

    firsts = [blk * width, (1 - blk) * width] if pair else [jnp.zeros_like(blk)]
    groups = [(k, k + 1) for k in range(0, chips, 2)] if chips % 2 == 0 else [(k,) for k in range(chips)]
    unit = 512 if hid % 512 == 0 else hid
    pos = jnp.stack(firsts).astype(jnp.int32)
    hidden, held = [], None
    for at, group in enumerate(groups):
        blocks = []
        for k in group:
            piece = arrived[k]
            own = [piece, to_blk(piece)] if pair else [lax.all_gather(piece, "blk", axis=1, tiled=True)]
            if at:
                own[-1] = after(own[-1], held)
            elif k == group[-1]:
                own[-1] = after(own[-1], scale, arrived[groups[-1][-1]])
            blocks += [own, [to_core(v) for v in own]]
        cuts = [0, hid]
        hidden.append([])
        for a, b in zip(cuts[:-1], cuts[1:]):
            hidden[-1].append(hidden_units(pos, blocks, w_gate, w_up, a, b, unit))
            pos = after(pos, hidden[-1][-1])
        held = hidden[-1][-1]

    over, sums = {}, {}

    def down(at, part, *earlier):
        group = groups[at]
        rows_of = [me ^ (CORES * k + core) for k in group for core in range(CORES)]
        where = jnp.stack([firsts[part]] + rows_of).astype(jnp.int32)
        outs = down_units(after(where, pos, *earlier), hidden[at], scale, w_down, tok, width)
        for i in range(len(group))[::-1]:
            total = outs[CORES * i].astype(f32) + to_core(outs[CORES * i + 1]).astype(f32)
            over[part, group[i]] = total.astype(bf16) if part else total
        return list(outs)

    if pair:
        came, done, last = {}, [], None
        for at in range(len(groups))[::-1]:
            done = down(at, 1, *done)
            if at == 0:
                gate = done[0]
            else:
                done = down(at, 0, *done) + [over[1, k] for k in groups[at]]
            for k in groups[at][::-1]:
                if k == chips - 1:
                    came[k] = to_blk(over[1, k])
                    last = sums[k] = (over[0, k] + came[k].astype(f32)).astype(bf16)
                elif at:
                    waiting = k
        k = waiting
        came[k] = to_blk(after(over[1, k], gate))
        down(0, 0, *done, last)
        sums[k] = over[0, k] + came[k].astype(f32)
        came[1] = to_blk(after(over[1, 1], last))
        sums[1] = over[0, 1] + came[1].astype(f32)
        came[0] = to_blk(after(over[1, 0], sums[2]))
        sums[0] = over[0, 0] + came[0].astype(f32)
    else:
        for at in range(len(groups)):
            down(at, 0)
        for k in range(chips):
            sums[k] = lax.psum_scatter(over[0, k], "blk", scatter_dimension=1, tiled=True)
    for bit in bits:
        for k in sorted(sums, reverse=True):
            if k & bit:
                sums[k ^ bit] = sums[k ^ bit] + to_chip(sums.pop(k).astype(bf16), bit).astype(f32)
    return sums[0].astype(bf16)


def solution(mesh):
    in_specs = (
        P(("groups", "expert"), "blk"),
        P(("groups", "expert"), None),
        P(("groups", "expert"), None),
        P(("expert", "blk"), None, None),
        P(("expert", "blk"), None, None),
        P(("expert", "blk"), None, None),
    )
    out_specs = P(("groups", "expert"), "blk")
    return jax.shard_map(
        on_device, mesh=mesh, in_specs=in_specs, out_specs=out_specs, check_vma=False
    )
```
